32 devices in a mesh: groups: 2 (over y), wide: 4 (over z), narrow: 2 (over x), vec: 2 (over core).
Axes of the slice: x: 2, y: 2, z: 4, core: 2. Of those that a mesh axis runs over, the one named last changes fastest.
Arguments:
- vectors: float32 [128, 128, 256], P(('groups', 'wide', 'narrow'), None, 'vec'), parts along dimension 0, may hold values from -6 to 6
- points: bfloat16 [128, 3, 256], P(('groups', 'wide', 'narrow')), parts along dimension 0, may hold values from 0 to 1
- near_list: int32 [128, 16], P(('groups', 'wide', 'narrow')), parts along dimension 0, may hold values from -1 to 63, as said below
- leaf_basis: bfloat16 [128, 64, 256], P(('groups', 'wide', 'narrow'), None, 'vec'), parts along dimension 0, may hold values from -0.375 to 0.375
- leaf_transfer: float32 [128, 64, 64], P(('groups', 'wide', 'narrow')), parts along dimension 0, may hold values from -0.75 to 0.75
- parent_to_cluster: float32 [16, 64, 64], P(('groups', 'wide', 'narrow')), parts along dimension 0, may hold values from -0.75 to 0.75
- skeleton: float32 [8, 3, 64], P('groups'), parts along dimension 0, may hold values from 0 to 1
- coupling: int32 [8, 2], P(('groups', 'wide')), parts along dimension 0, may hold values from 0 to 3, as said below
Outputs:
- product: float32 [128, 128, 256], P(('groups', 'wide', 'narrow'), None, 'vec'), parts along dimension 0
The draws below stay inside these ranges and needn't reach their ends.
There are 2 independent parts, one for each index of `groups`. The reference program is written for one: setup_inputs(seed, part) draws one part's arguments, and reference() takes and returns one part's arrays. A program takes and returns all parts, laid end to end along the dimension named above; each array names one. Nothing has to cross between parts.
Inputs may be any that keep to these rules, and one draw needn't show every extreme that they name: `near_list`: entry 0 of a row is the row's own leaf; the used entries of a row are distinct leaves, at least two, and -1 fills the unused slots after them. Among the rows of one device (aligned blocks of 8 rows), at most 4 distinct leaves lie in any one other cluster of 16 leaves, and every device reaches 4 for some cluster. `coupling`: each row names 2 distinct clusters other than its own.
All inputs are finite; a program needn't handle non-finite values.
Results may differ from the reference program's by a relative error of at most 0.0045.
Values may be sent and summed in bfloat16 or wider, within the bound.
A program may use at most 64 MiB of HBM per device.

```python
import jax
import jax.numpy as jnp
from jax import lax

LEAF = 256
RANK = 64
RHS_COLUMNS = 128
LEAF_DEV = 8
SEND_CAP = 4
LOCAL_NEAR = 12
CLUSTERS = 4
BLOCK_LEAVES = 16
LEAVES = 64
PARENTS = 8
REMOTE_NEAR = 3
NEAR_SLOTS = 16
COUPLED = 2


def draw_near_list(key, part):
    key = jax.random.fold_in(key, 11)
    keys = jax.random.split(key, 7)
    device_total = LEAVES // LEAF_DEV
    leaf_ids = jnp.arange(LEAVES, dtype=jnp.int32)
    device_of = leaf_ids // LEAF_DEV
    block_of = leaf_ids // BLOCK_LEAVES
    within = leaf_ids % BLOCK_LEAVES
    position = leaf_ids % LEAF_DEV
    main_offset = jax.random.randint(keys[0], (device_total,), 1, CLUSTERS)
    pool_keys = jax.random.split(keys[1], device_total * CLUSTERS)
    pools = jax.vmap(lambda subkey: jax.random.permutation(subkey, BLOCK_LEAVES)[:SEND_CAP])(pool_keys)
    pools = pools.reshape(device_total, CLUSTERS, SEND_CAP)
    main_block = (block_of + main_offset[device_of]) % CLUSTERS
    main_leaf = main_block * BLOCK_LEAVES + pools[device_of, main_block, position % SEND_CAP]
    local_keys = jax.random.split(keys[2], LEAVES)
    local_offset = 1 + jax.vmap(lambda subkey: jax.random.permutation(subkey, BLOCK_LEAVES - 1)[:LOCAL_NEAR])(local_keys)
    local_leaf = block_of[:, None] * BLOCK_LEAVES + (within[:, None] + local_offset) % BLOCK_LEAVES
    other_keys = jax.random.split(keys[3], LEAVES)
    selected_option = jax.vmap(lambda subkey: jax.random.permutation(subkey, CLUSTERS - 2)[:REMOTE_NEAR - 1])(other_keys)
    skipped = (1 + selected_option >= main_offset[device_of][:, None]).astype(jnp.int32)
    other_block = (block_of[:, None] + 1 + selected_option + skipped) % CLUSTERS
    pool_slot = jax.random.randint(keys[4], (LEAVES, REMOTE_NEAR - 1), 0, SEND_CAP)
    other_leaf = other_block * BLOCK_LEAVES + pools[device_of[:, None], other_block, pool_slot]
    entries = jnp.concatenate([leaf_ids[:, None], main_leaf[:, None], local_leaf, other_leaf], axis=1)
    density = jax.random.randint(keys[5], (device_total,), 0, 4)
    spread = jax.random.randint(keys[6], (LEAVES,), 0, NEAR_SLOTS - 1)
    used_count = 2 + spread * (1 + density[device_of]) // 4
    used = jnp.arange(NEAR_SLOTS)[None, :] < used_count[:, None]
    return jnp.where(used, entries, -1).astype(jnp.int32)


def draw_skeleton(key, part):
    key = jax.random.fold_in(key, 37)
    keys = jax.random.split(key, 2)
    index = jnp.arange(RANK)
    lattice = jnp.stack([index % 4, index // 4 % 4, index // 16 % 4]).astype(jnp.float32)
    offset = jax.random.uniform(keys[0], (CLUSTERS, 3, 1), jnp.float32, 0.0, 0.04)
    jitter = jnp.clip(0.015 * jax.random.normal(keys[1], (CLUSTERS, 3, RANK), jnp.float32), -0.03, 0.03)
    return (0.03 + 0.3 * lattice[None] + offset + jitter).astype(jnp.float32)


def draw_coupling(key, part):
    key = jax.random.fold_in(key, 23)
    keys = jax.random.split(key, CLUSTERS)
    selected_option = jax.vmap(lambda subkey: jax.random.permutation(subkey, CLUSTERS - 1)[:COUPLED])(keys)
    return ((jnp.arange(CLUSTERS)[:, None] + 1 + selected_option) % CLUSTERS).astype(jnp.int32)


def block_levels(rng, extent, pieces, least, largest):
    factor_of = 1.0
    for dim, parts in pieces:
        draws = jax.random.uniform(jax.random.fold_in(jax.random.fold_in(rng, 6), dim), (parts,), jnp.float32, least / len(pieces), largest / len(pieces))
        factor_of = factor_of * jnp.repeat(jnp.exp(draws), extent[dim] // parts).reshape((-1,) + (1,) * (len(extent) - 1 - dim))
    return factor_of


def centred(stream_key, extent, scale, bound, pieces=(), kind=jnp.bfloat16):
    drawn = jax.random.normal(stream_key, extent, jnp.float32) * scale
    if len(pieces) > 0:
        drawn = block_levels(stream_key, extent, pieces, -0.22, 0.18) * drawn
    return jnp.clip(drawn, min=-bound, max=bound).astype(kind)


def setup_inputs(seed: int = 0, part: int = 0) -> dict:
    key_list = jax.random.split(jax.random.key(seed), 9)
    part_splits = jax.random.split(jax.random.fold_in(key_list[8], part), 9)
    vectors = centred(part_splits[0], (LEAVES, RHS_COLUMNS, LEAF), 1.0, 6.0, ((0, 8), (2, 2)), jnp.float32)
    points = jnp.clip(1.0 * jax.random.uniform(part_splits[1], (LEAVES, 3, LEAF), jnp.float32) ** block_levels(part_splits[1], (LEAVES, 3, LEAF), ((0, 8),), -0.2, 0.2), 0.0, 1.0).astype(jnp.bfloat16)
    near_list = draw_near_list(jax.random.fold_in(jax.random.fold_in(key_list[8], part), 71), part)
    leaf_basis = centred(part_splits[3], (LEAVES, RANK, LEAF), LEAF ** -0.5, 0.375, ((0, 8), (2, 2)))
    leaf_transfer = centred(part_splits[4], (LEAVES, RANK, RANK), RANK ** -0.5, 0.75, ((0, 8),), jnp.float32)
    parent_to_cluster = centred(part_splits[5], (PARENTS, RANK, RANK), RANK ** -0.5, 0.75, ((0, 8),), jnp.float32)
    skeleton = draw_skeleton(jax.random.fold_in(jax.random.fold_in(key_list[8], part), 71), part)
    coupling = draw_coupling(jax.random.fold_in(jax.random.fold_in(key_list[8], part), 71), part)
    return dict(vectors=vectors, points=points, near_list=near_list, leaf_basis=leaf_basis, leaf_transfer=leaf_transfer, parent_to_cluster=parent_to_cluster, skeleton=skeleton, coupling=coupling)


kernel_rate = 8.660254037844386
signal = 0.125
finest_level = lax.Precision.HIGHEST

def matern_kernel(source_pts, target_pts):
    first = source_pts.astype(jnp.float32)
    second = target_pts.astype(jnp.float32)
    delta_x = first[..., 0, :, None] - second[..., 0, None, :]
    delta_y = first[..., 1, :, None] - second[..., 1, None, :]
    delta_z = first[..., 2, :, None] - second[..., 2, None, :]
    squared = delta_x * delta_x + delta_y * delta_y + delta_z * delta_z
    scaled = kernel_rate * jnp.sqrt(squared)
    return signal * (1.0 + scaled) * jnp.exp(-scaled)

def reference(vectors, points, near_list, leaf_basis, leaf_transfer, parent_to_cluster, skeleton, coupling):
    rounded = vectors.astype(jnp.bfloat16)
    rounded_wide = lax.optimization_barrier(rounded).astype(jnp.float32)

    def near_one(leaf_item):
        entries, own_pts = leaf_item
        usable = (entries >= 0).astype(jnp.float32)
        clamped = jnp.maximum(entries, 0).astype(jnp.int32)
        sources = jnp.take(rounded_wide, clamped, axis=0)
        kernel_tile = matern_kernel(jnp.take(points, clamped, axis=0), own_pts[None]) * usable[:, None, None]
        kernel_tile = lax.optimization_barrier(kernel_tile.astype(jnp.bfloat16)).astype(jnp.float32)
        return jnp.einsum('kcs,ksu->cu', sources, kernel_tile, precision=finest_level)
    near_part = lax.map(near_one, (near_list, points))
    basis_wide = leaf_basis.astype(jnp.float32)
    leaf_weights = jnp.einsum('lcp,lrp->lcr', rounded_wide, basis_wide, precision=finest_level)
    leaf_weights = leaf_weights.reshape(PARENTS, LEAF_DEV, RHS_COLUMNS, RANK)
    transfer_grouped = leaf_transfer.reshape(PARENTS, LEAF_DEV, RANK, RANK)
    parent_weight_sums = jnp.einsum('plcr,plrq->pcq', leaf_weights, transfer_grouped, precision=finest_level)
    parent_contributions = jnp.einsum('idl,ilj->idj', parent_weight_sums, parent_to_cluster, precision=finest_level)
    per_cluster = PARENTS // CLUSTERS
    root_weight_values = lax.optimization_barrier(jnp.sum(parent_contributions.reshape(CLUSTERS, per_cluster, RHS_COLUMNS, RANK), axis=1))
    sources_top = jnp.take(root_weight_values, coupling, axis=0)
    coupling_tile = matern_kernel(jnp.take(skeleton, coupling, axis=0), skeleton[:, None])
    top_fields = jnp.einsum('gkcr,gkrq->gcq', sources_top, coupling_tile, precision=finest_level)
    parent_grouped = parent_to_cluster.reshape(CLUSTERS, per_cluster, RANK, RANK)
    parent_fields = jnp.einsum('gcq,gprq->gpcr', top_fields, parent_grouped, precision=finest_level)
    parent_fields = parent_fields.reshape(PARENTS, RHS_COLUMNS, RANK)
    leaf_fields = jnp.einsum('pcq,plrq->plcr', parent_fields, transfer_grouped, precision=finest_level)
    leaf_fields = leaf_fields.reshape(LEAVES, RHS_COLUMNS, RANK).astype(jnp.bfloat16)
    leaf_fields = lax.optimization_barrier(leaf_fields).astype(jnp.float32)
    far_part = jnp.einsum('lcr,lrp->lcp', leaf_fields, basis_wide, precision=finest_level)
    return vectors + near_part + far_part
```

```python
import functools
import math

import jax
import jax.numpy as jnp
from jax import lax
from jax.experimental import pallas as pl
from jax.experimental.pallas import tpu as pltpu
from jax.sharding import PartitionSpec as P

SEND_CAP = 4
FEATS = 16
CHUNKS = 2

RATE = 8.660254037844386
LOG2E = math.log2(math.e)
LN2 = math.log(2.0)
SCALE = (RATE * LOG2E) ** 2
MESH = pl.DeviceIdType.MESH
HIGH = lax.Precision.HIGHEST
F32, BF16, I32 = jnp.float32, jnp.bfloat16, jnp.int32


def each(count, step):
    if count <= 8:
        for i in range(count):
            step(i)
    else:
        lax.fori_loop(0, count, lambda i, _: (step(i), 0)[1], 0)


def pieces(value):
    first = value.astype(BF16).astype(F32)
    rest = value - first
    second = rest.astype(BF16).astype(F32)
    return [first, second, rest - second]


def dot(a, b, ca=1, cb=0, precision=None):
    return lax.dot_general(
        a, b, (((ca,), (cb,)), ((), ())), precision=precision, preferred_element_type=F32
    )


def kernel(
    W, N, V,
    vec_ref, pts_ref, near_s, near_v, basis_ref, lt_ref, ptc_ref, skel_ref, coup_s,
    out_ref, *scratch,
):
    ch = CHUNKS
    loc, cand, scratch = scratch[:ch], scratch[ch : 2 * ch], scratch[2 * ch :]
    (
        stage, req_out, req_in, req_s, map_v, map_s, pts_out, pts_in, feat, bfeat, tiles,
        term, mate_in, top_all, fpiece, field, near_out, near_in, near_acc,
        s_req, r_req, s_pts, r_pts, s_nar, r_nar, s_wide, r_wide,
        s_mate, r_mate, s_top, r_top, s_ag, r_ag, s_near, r_near, l_req, l_map,
    ) = scratch
    ld, cols, half = vec_ref.shape
    full = pts_ref.shape[2]
    slots = near_v.shape[1]
    cw = cols // ch
    block = ld * N
    leaves = W * block
    shift = block.bit_length() - 1
    lp = max(128, leaves)
    mates = N * V
    pr = cols // mates
    w, n, v = lax.axis_index("wide"), lax.axis_index("narrow"), lax.axis_index("vec")
    me = n * V + v

    def mate(d):
        m = lax.rem(me + d, mates)
        return {"narrow": m // V, "vec": m % V}

    def wide_peer(d):
        return {"wide": lax.rem(w + d, W)}

    def narrow_peer(d):
        return {"narrow": lax.rem(n + d, N)}

    spot = w * N + n

    def group_peer(d):
        p = lax.rem(spot + d, W * N)
        return {"wide": p // N, "narrow": p % N}

    other = {"vec": 1 - v}

    def rcopy(src, dst, ss, rs, dev):
        return pltpu.make_async_remote_copy(
            src_ref=src, dst_ref=dst, send_sem=ss, recv_sem=rs, device_id=dev, device_id_type=MESH
        )

    barrier = pltpu.get_barrier_semaphore()

    def greet(fn):
        def step(i):
            pl.semaphore_signal(barrier, inc=1, device_id=fn(i + 1), device_id_type=MESH)
        return step

    each(W * N - 1, greet(group_peer))
    each(mates - 1, greet(mate))

    base = n * ld
    for c in range(ch):
        loc[c][pl.ds(base, ld)] = vec_ref[:, c * cw : (c + 1) * cw, :].astype(BF16)
        cand[c][pl.ds(block + w * SEND_CAP, SEND_CAP)] = jnp.zeros((SEND_CAP, cw, half), BF16)

    nl = near_v[...]
    lane = lax.broadcasted_iota(I32, (ld, lp), 1)
    hits = jnp.zeros((ld, lp), F32)
    for k in range(slots):
        hits = jnp.where(nl[:, k : k + 1] == lane, 1.0, hits)
    mask = jnp.broadcast_to(jnp.max(hits, axis=0, keepdims=True), (8, lp))
    lane8 = lax.broadcasted_iota(I32, (8, lp), 1)
    owner8 = lax.shift_right_logical(lane8, shift)
    mask = jnp.where(owner8 == w, 0.0, mask)
    ti = lax.broadcasted_iota(I32, (lp, lp), 0)
    tj = lax.broadcasted_iota(I32, (lp, lp), 1)
    tri = (ti < tj) & (lax.shift_right_logical(ti, shift) == lax.shift_right_logical(tj, shift))
    rank = dot(mask.astype(BF16), jnp.where(tri, 1.0, 0.0).astype(BF16))
    row8 = lax.broadcasted_iota(I32, (8, lp), 0).astype(F32)
    inner8 = (lane8 & (block - 1)).astype(F32)
    sel = jnp.where((rank == row8) & (mask > 0.5), inner8, 0.0)
    si = lax.broadcasted_iota(I32, (lp, 128), 0)
    sj = lax.broadcasted_iota(I32, (lp, 128), 1)
    seg = jnp.where(lax.shift_right_logical(si, shift) == sj, 1.0, 0.0).astype(BF16)
    req_out[...] = dot(sel.astype(BF16), seg).astype(I32)

    pts = pts_ref[...].astype(F32)
    xyz = [pts[:, c, :] for c in range(3)]
    halves = [jnp.where(v == 0, a[:, :half], a[:, half:]) for a in xyz]
    prow = pts_out.shape[0]
    pts_out[...] = jnp.concatenate(
        halves + [jnp.zeros((prow - 3 * ld, half), F32)], axis=0
    ).astype(BF16)
    pts_in[pl.ds(spot, 1)] = pts_out[...][None]

    weights = [
        dot(
            jnp.concatenate([loc[c][base + l] for c in range(ch)], axis=0), basis_ref[l], 1, 1
        )
        for l in range(ld)
    ]
    sums = weights[0] * 0.0
    for l in range(ld):
        sums = sums + dot(weights[l], lt_ref[l], precision=HIGH)
    term[...] = dot(sums, ptc_ref[0], precision=HIGH).reshape(mates, pr, -1)

    pl.semaphore_wait(barrier, W * N - 1 + mates - 1)

    def req_copy(i):
        return rcopy(req_out, req_in.at[i], s_req.at[i], r_req.at[i], wide_peer(i + 1))

    def mate_copy(i):
        m = lax.rem(me + i + 1, mates)
        return rcopy(term.at[m], mate_in.at[i], s_mate.at[i], r_mate.at[i], mate(i + 1))

    def pts_copy(i):
        return rcopy(pts_out, pts_in.at[spot], s_pts.at[i], r_pts.at[i], group_peer(i + 1))

    def nar_copy(i, c):
        mine = loc[c].at[pl.ds(base, ld)]
        return rcopy(mine, mine, s_nar.at[c, i], r_nar.at[c, i], narrow_peer(i + 1))

    each(W - 1, lambda i: req_copy(i).start())
    each(mates - 1, lambda i: mate_copy(i).start())
    each(W * N - 1, lambda i: pts_copy(i).start())
    for c in range(ch):
        each(N - 1, lambda i: nar_copy(i, c).start())

    owner_l = lax.shift_right_logical(lane, shift)
    place = jnp.where(
        owner_l == w,
        (lane - w * block).astype(F32),
        (block + owner_l * SEND_CAP).astype(F32) + jnp.broadcast_to(rank[:1], (ld, lp)),
    )
    mlane = lax.broadcasted_iota(I32, (ld, 128), 1)
    found = jnp.zeros((ld, 128), F32)
    zero_slot = (block + w * SEND_CAP).astype(F32)
    for k in range(slots):
        entry = nl[:, k : k + 1]
        at = jnp.sum(jnp.where(entry == lane, place, 0.0), axis=1, keepdims=True)
        at = jnp.where(entry >= 0, at, zero_slot)
        found = jnp.where(mlane == k, at, found)
    map_v[...] = found.astype(I32)
    map_copy = pltpu.make_async_copy(map_v, map_s, l_map)
    map_copy.start()

    rows = ld * FEATS
    pi = lax.broadcasted_iota(I32, (rows, rows), 0)
    pj = lax.broadcasted_iota(I32, (rows, rows), 1)
    fshift = FEATS.bit_length() - 1
    perm = pj == (pi & (FEATS - 1)) * ld + lax.shift_right_logical(pi, fshift)
    perm = jnp.where(perm, 1.0, 0.0).astype(BF16)
    one_b = jnp.ones((ld, full), F32)
    norm = (xyz[0] * xyz[0] + xyz[1] * xyz[1] + xyz[2] * xyz[2]) * SCALE
    brows = sum((pieces(a * (-2.0 * SCALE)) for a in xyz), [])
    brows = brows + [one_b] * 3 + pieces(norm) + [one_b * 0.0]
    bfeat[...] = (
        dot(perm, jnp.concatenate(brows, axis=0).astype(BF16))
        .astype(BF16)
        .reshape(ld, FEATS, full)
    )

    each(mates - 1, lambda i: mate_copy(i).wait_recv())
    mine = term[me]
    for i in range(mates - 1):
        mine = mine + mate_in[i]
    top_all[pl.ds(w, 1)] = mine[None]

    def top_copy(i):
        t = top_all.at[w]
        return rcopy(t, t, s_top.at[i], r_top.at[i], wide_peer(i + 1))

    each(W - 1, lambda i: top_copy(i).start())

    each(W - 1, lambda i: req_copy(i).wait_recv())
    req_local = pltpu.make_async_copy(req_in, req_s, l_req)
    req_local.start()
    req_local.wait()

    def wide_copy(i, c):
        return rcopy(
            stage.at[c, i], cand[c].at[pl.ds(block + w * SEND_CAP, SEND_CAP)],
            s_wide.at[c, i], r_wide.at[c, i], wide_peer(i + 1),
        )

    for c in range(ch):
        each(N - 1, lambda i: nar_copy(i, c).wait_recv())

        def put(i):
            for r in range(SEND_CAP):
                leaf = jnp.clip(req_s[i, r, w], 0, block - 1)
                stage[c, W - 2 - i, r] = loc[c][leaf]

        each(W - 1, put)
        each(W - 1, lambda i: wide_copy(i, c).start())
        cand[c][pl.ds(0, block)] = loc[c][...]

    each(W * N - 1, lambda i: pts_copy(i).wait_recv())

    def features(i):
        a = pts_in[i].astype(F32)
        abc = [a[c * ld : (c + 1) * ld] for c in range(3)]
        anorm = (abc[0] * abc[0] + abc[1] * abc[1] + abc[2] * abc[2]) * SCALE
        one_a = jnp.ones((ld, half), F32)
        arows = [abc[0]] * 3 + [abc[1]] * 3 + [abc[2]] * 3
        arows = arows + pieces(anorm) + [one_a] * 3 + [one_a * 0.0]
        feat[pl.ds(i * ld, ld)] = (
            dot(perm, jnp.concatenate(arows, axis=0).astype(BF16))
            .astype(BF16)
            .reshape(ld, FEATS, half)
        )

    each(W * N, features)

    def make_tiles(first, last):
        def step(t, carry):
            b = bfeat[t]
            for k in range(slots):
                a = feat[jnp.maximum(near_s[t, k], 0)]
                s = jnp.maximum(dot(a, b, 0, 0), 1e-30)
                q = s * lax.rsqrt(s)
                tile = (1.0 + LN2 * q) * jnp.exp2(-q)
                tiles[t, k * half : (k + 1) * half, :] = tile.astype(BF16)
            return carry

        lax.fori_loop(first, last, step, 0)

    cut = ld // 2
    make_tiles(0, cut)

    each(W - 1, lambda i: top_copy(i).wait_recv())
    rank_dim = skel_ref.shape[2]
    own = skel_ref[w]
    fields = jnp.zeros((pr, rank_dim), F32)
    for k in range(coup_s.shape[1]):
        partner = coup_s[0, k]
        src = skel_ref[partner]
        sq = jnp.zeros((rank_dim, rank_dim), F32)
        for c in range(3):
            col = jnp.broadcast_to(src[c : c + 1, :], (rank_dim, rank_dim)).T
            delta = col - own[c : c + 1, :]
            sq = sq + delta * delta
        q = RATE * jnp.sqrt(sq)
        tile = 0.125 * (1.0 + q) * jnp.exp(-q)
        fields = fields + dot(top_all[partner], tile, precision=HIGH)
    fpiece[pl.ds(me, 1)] = fields[None]

    def ag_copy(i):
        f = fpiece.at[me]
        return rcopy(f, f, s_ag.at[i], r_ag.at[i], mate(i + 1))

    each(mates - 1, lambda i: ag_copy(i).start())
    make_tiles(cut, ld)
    each(mates - 1, lambda i: ag_copy(i).wait_recv())

    top = fpiece[...].reshape(cols, rank_dim)
    parent = dot(top, ptc_ref[0], 1, 1, precision=HIGH)
    for l in range(ld):
        lf = dot(parent, lt_ref[l], 1, 1, precision=HIGH).astype(BF16)
        out_ref[l] = vec_ref[l] + dot(lf, basis_ref[l])

    map_copy.wait()

    def near_copy(c, t):
        return rcopy(
            near_out.at[c, t], near_in.at[c, t], s_near.at[c, t], r_near.at[c, t], other
        )

    for c in range(ch):
        each(W - 1, lambda i: wide_copy(i, c).wait_recv())

        def product(t, carry):
            acc = jnp.zeros((cw, full), F32)
            for k in range(0, slots, 2):
                at = [jnp.clip(map_s[t, k + j], 0, block + W * SEND_CAP - 1) for j in range(2)]
                lhs = jnp.concatenate([cand[c][at[0]], cand[c][at[1]]], axis=1)
                acc = acc + dot(lhs, tiles[t, k * half : (k + 2) * half, :])
            acc = acc * 0.125
            low, high = acc[:, :half], acc[:, half:]
            near_acc[t, c * cw : (c + 1) * cw, :] = jnp.where(v == 0, low, high)
            near_out[c, t] = jnp.where(v == 0, high, low).astype(BF16)
            near_copy(c, t).start()
            return carry

        lax.fori_loop(0, ld, product, 0)

    for c in range(ch):
        def finish(t, carry):
            near_copy(c, t).wait_recv()
            rows_c = slice(c * cw, (c + 1) * cw)
            out_ref[t, rows_c, :] = (
                out_ref[t, rows_c, :] + near_acc[t, rows_c, :] + near_in[c, t].astype(F32)
            )
            return carry

        lax.fori_loop(0, ld, finish, 0)

    each(W - 1, lambda i: req_copy(i).wait_send())
    each(mates - 1, lambda i: mate_copy(i).wait_send())
    each(W * N - 1, lambda i: pts_copy(i).wait_send())
    each(W - 1, lambda i: top_copy(i).wait_send())
    each(mates - 1, lambda i: ag_copy(i).wait_send())
    for c in range(ch):
        each(N - 1, lambda i: nar_copy(i, c).wait_send())
        each(W - 1, lambda i: wide_copy(i, c).wait_send())
        each(ld, lambda t: near_copy(c, t).wait_send())


def body(W, N, V, vectors, points, near_list, basis, transfer, ptc, skeleton, coupling):
    ld, cols, half = vectors.shape
    full = points.shape[2]
    slots = near_list.shape[1]
    rank = transfer.shape[1]
    ch = CHUNKS
    cw = cols // ch
    block = ld * N
    mates = N * V
    pr = cols // mates
    prow = -(-3 * ld // 16) * 16
    dma = pltpu.SemaphoreType.DMA
    vmem = pltpu.VMEM
    scratch = [vmem((block, cw, half), BF16)] * ch
    scratch += [vmem((block + W * SEND_CAP, cw, half), BF16)] * ch
    scratch += [
        vmem((ch, W - 1, SEND_CAP, cw, half), BF16),
        vmem((8, 128), I32),
        vmem((W - 1, 8, 128), I32),
        pltpu.SMEM((W - 1, 8, 128), I32),
        vmem((ld, 128), I32),
        pltpu.SMEM((ld, 128), I32),
        vmem((prow, half), BF16),
        vmem((W * N, prow, half), BF16),
        vmem((W * N * ld, FEATS, half), BF16),
        vmem((ld, FEATS, full), BF16),
        vmem((ld, slots * half, full), BF16),
        vmem((mates, pr, rank), F32),
        vmem((mates - 1, pr, rank), F32),
        vmem((W, pr, rank), F32),
        vmem((mates, pr, rank), F32),
        vmem((8, 128), F32),
        vmem((ch, ld, cw, half), BF16),
        vmem((ch, ld, cw, half), BF16),
        vmem((ld, cols, half), F32),
    ]
    scratch += [dma((W - 1,))] * 2 + [dma((W * N - 1,))] * 2 + [dma((ch, N - 1))] * 2
    scratch += [dma((ch, W - 1))] * 2 + [dma((mates - 1,))] * 2 + [dma((W - 1,))] * 2
    scratch += [dma((mates - 1,))] * 2 + [dma((ch, ld))] * 2 + [dma(())] * 2
    in_v = pl.BlockSpec(memory_space=pltpu.VMEM)
    in_s = pl.BlockSpec(memory_space=pltpu.SMEM)
    return pl.pallas_call(
        functools.partial(kernel, W, N, V),
        out_shape=jax.ShapeDtypeStruct(vectors.shape, F32),
        in_specs=[in_v, in_v, in_s, in_v, in_v, in_v, in_v, in_v, in_s],
        out_specs=in_v,
        scratch_shapes=scratch,
        compiler_params=pltpu.CompilerParams(
            collective_id=0, has_side_effects=True, vmem_limit_bytes=56 << 20
        ),
    )(vectors, points, near_list, near_list, basis, transfer, ptc, skeleton, coupling)


def solution(mesh):
    rows = ("groups", "wide", "narrow")
    in_specs = (
        P(rows, None, "vec"),
        P(rows, None, None),
        P(rows, None),
        P(rows, None, "vec"),
        P(rows, None, None),
        P(rows, None, None),
        P("groups", None, None),
        P(("groups", "wide"), None),
    )
    sizes = [mesh.shape[a] for a in ("wide", "narrow", "vec")]
    return jax.shard_map(
        functools.partial(body, *sizes),
        mesh=mesh,
        in_specs=in_specs,
        out_specs=P(rows, None, "vec"),
        check_vma=False,
    )
```

```python
import functools
import math

import jax
import jax.numpy as jnp
from jax import lax
from jax.experimental import pallas as pl
from jax.experimental.pallas import tpu as pltpu
from jax.sharding import PartitionSpec as P

SEND_CAP = 4
FEATS = 16
CHUNKS = 4

RATE = 8.660254037844386
LOG2E = math.log2(math.e)
LN2 = math.log(2.0)
SCALE = (RATE * LOG2E) ** 2
MESH = pl.DeviceIdType.MESH
HIGH = lax.Precision.HIGHEST
F32, BF16, I32 = jnp.float32, jnp.bfloat16, jnp.int32


def each(count, step):
    if count <= 8:
        for i in range(count):
            step(i)
    else:
        lax.fori_loop(0, count, lambda i, _: (step(i), 0)[1], 0)


def pieces(value):
    first = value.astype(BF16).astype(F32)
    rest = value - first
    second = rest.astype(BF16).astype(F32)
    return [first, second, rest - second]


def dot(a, b, ca=1, cb=0, precision=None):
    return lax.dot_general(
        a, b, (((ca,), (cb,)), ((), ())), precision=precision, preferred_element_type=F32
    )


def kernel(
    W, N, V,
    vec_ref, pts_ref, near_s, near_v, basis_ref, lt_ref, ptc_ref, skel_ref, coup_s,
    out_ref, *scratch,
):
    ch = CHUNKS
    loc, cand, scratch = scratch[:ch], scratch[ch : 2 * ch], scratch[2 * ch :]
    (
        stage, req_out, req_in, req_s, map_v, map_s, pts_out, pts_in, feat, bfeat, tiles,
        term, mate_in, top_all, fpiece, near_out, near_in,
        s_req, r_req, s_pts, r_pts, s_nar, r_nar, s_wide, r_wide,
        s_mate, r_mate, s_top, r_top, s_ag, r_ag, s_near, r_near, l_req, l_map,
    ) = scratch
    ld, cols, half = vec_ref.shape
    full = pts_ref.shape[2]
    slots = near_v.shape[1]
    cw = cols // ch
    block = ld * N
    leaves = W * block
    shift = block.bit_length() - 1
    lp = max(128, leaves)
    mates = N * V
    pr = cols // mates
    w, n, v = lax.axis_index("wide"), lax.axis_index("narrow"), lax.axis_index("vec")
    me = n * V + v

    def mate(d):
        m = lax.rem(me + d, mates)
        return {"narrow": m // V, "vec": m % V}

    def wide_peer(d):
        return {"wide": lax.rem(w + d, W)}

    def narrow_peer(d):
        return {"narrow": lax.rem(n + d, N)}

    spot = w * N + n

    def group_peer(d):
        p = lax.rem(spot + d, W * N)
        return {"wide": p // N, "narrow": p % N}

    other = {"vec": 1 - v}

    def rcopy(src, dst, ss, rs, dev):
        return pltpu.make_async_remote_copy(
            src_ref=src, dst_ref=dst, send_sem=ss, recv_sem=rs, device_id=dev, device_id_type=MESH
        )

    barrier = pltpu.get_barrier_semaphore()

    def greet(fn):
        def step(i):
            pl.semaphore_signal(barrier, inc=1, device_id=fn(i + 1), device_id_type=MESH)
        return step

    each(W * N - 1, greet(group_peer))
    each(mates - 1, greet(mate))

    base = n * ld
    for c in range(ch):
        loc[c][pl.ds(base, ld)] = vec_ref[:, c * cw : (c + 1) * cw, :].astype(BF16)
        cand[c][pl.ds(block + w * SEND_CAP, SEND_CAP)] = jnp.zeros((SEND_CAP, cw, half), BF16)

    nl = near_v[...]
    lane = lax.broadcasted_iota(I32, (ld, lp), 1)
    hits = jnp.zeros((ld, lp), F32)
    for k in range(slots):
        hits = jnp.where(nl[:, k : k + 1] == lane, 1.0, hits)
    mask = jnp.broadcast_to(jnp.max(hits, axis=0, keepdims=True), (8, lp))
    lane8 = lax.broadcasted_iota(I32, (8, lp), 1)
    owner8 = lax.shift_right_logical(lane8, shift)
    mask = jnp.where(owner8 == w, 0.0, mask)
    ti = lax.broadcasted_iota(I32, (lp, lp), 0)
    tj = lax.broadcasted_iota(I32, (lp, lp), 1)
    tri = (ti < tj) & (lax.shift_right_logical(ti, shift) == lax.shift_right_logical(tj, shift))
    rank = dot(mask.astype(BF16), jnp.where(tri, 1.0, 0.0).astype(BF16))
    row8 = lax.broadcasted_iota(I32, (8, lp), 0).astype(F32)
    inner8 = (lane8 & (block - 1)).astype(F32)
    sel = jnp.where((rank == row8) & (mask > 0.5), inner8, 0.0)
    si = lax.broadcasted_iota(I32, (lp, 128), 0)
    sj = lax.broadcasted_iota(I32, (lp, 128), 1)
    seg = jnp.where(lax.shift_right_logical(si, shift) == sj, 1.0, 0.0).astype(BF16)
    req_out[...] = dot(sel.astype(BF16), seg).astype(I32)

    xyz = [pts_ref[c].astype(F32) for c in range(3)]
    halves = [jnp.where(v == 0, a[:, :half], a[:, half:]) for a in xyz]
    prow = pts_out.shape[0]
    pts_out[...] = jnp.concatenate(
        halves + [jnp.zeros((prow - 3 * ld, half), F32)], axis=0
    ).astype(BF16)
    pts_in[pl.ds(spot, 1)] = pts_out[...][None]

    weights = [
        dot(
            jnp.concatenate([loc[c][base + l] for c in range(ch)], axis=0), basis_ref[l], 1, 1
        )
        for l in range(ld)
    ]
    sums = weights[0] * 0.0
    for l in range(ld):
        sums = sums + dot(weights[l], lt_ref[l], precision=HIGH)
    term[...] = dot(sums, ptc_ref[0], precision=HIGH).reshape(mates, pr, -1)

    pl.semaphore_wait(barrier, W * N - 1 + mates - 1)

    def req_copy(i):
        return rcopy(req_out, req_in.at[i], s_req.at[i], r_req.at[i], wide_peer(i + 1))

    def mate_copy(i):
        m = lax.rem(me + i + 1, mates)
        return rcopy(term.at[m], mate_in.at[i], s_mate.at[i], r_mate.at[i], mate(i + 1))

    def pts_copy(i):
        return rcopy(pts_out, pts_in.at[spot], s_pts.at[i], r_pts.at[i], group_peer(i + 1))

    def nar_copy(i, c):
        mine = loc[c].at[pl.ds(base, ld)]
        return rcopy(mine, mine, s_nar.at[c, i], r_nar.at[c, i], narrow_peer(i + 1))

    each(W - 1, lambda i: req_copy(i).start())
    each(mates - 1, lambda i: mate_copy(i).start())
    each(W * N - 1, lambda i: pts_copy(i).start())
    for c in range(ch):
        each(N - 1, lambda i: nar_copy(i, c).start())

    owner_l = lax.shift_right_logical(lane, shift)
    place = jnp.where(
        owner_l == w,
        (lane - w * block).astype(F32),
        (block + owner_l * SEND_CAP).astype(F32) + jnp.broadcast_to(rank[:1], (ld, lp)),
    )
    mlane = lax.broadcasted_iota(I32, (ld, 128), 1)
    found = jnp.zeros((ld, 128), F32)
    zero_slot = (block + w * SEND_CAP).astype(F32)
    for k in range(slots):
        entry = nl[:, k : k + 1]
        at = jnp.sum(jnp.where(entry == lane, place, 0.0), axis=1, keepdims=True)
        at = jnp.where(entry >= 0, at, zero_slot)
        found = jnp.where(mlane == k, at, found)
    map_v[...] = found.astype(I32)
    map_copy = pltpu.make_async_copy(map_v, map_s, l_map)
    map_copy.start()

    rows = ld * FEATS
    pi = lax.broadcasted_iota(I32, (rows, rows), 0)
    pj = lax.broadcasted_iota(I32, (rows, rows), 1)
    fshift = FEATS.bit_length() - 1
    perm = pj == (pi & (FEATS - 1)) * ld + lax.shift_right_logical(pi, fshift)
    perm = jnp.where(perm, 1.0, 0.0).astype(BF16)
    one_b = jnp.ones((ld, full), F32)
    norm = (xyz[0] * xyz[0] + xyz[1] * xyz[1] + xyz[2] * xyz[2]) * SCALE
    brows = sum((pieces(a * (-2.0 * SCALE)) for a in xyz), [])
    brows = brows + [one_b] * 3 + pieces(norm) + [one_b * 0.0]
    bfeat[...] = (
        dot(perm, jnp.concatenate(brows, axis=0).astype(BF16))
        .astype(BF16)
        .reshape(ld, FEATS, full)
    )

    each(mates - 1, lambda i: mate_copy(i).wait_recv())
    mine = term[me]
    for i in range(mates - 1):
        mine = mine + mate_in[i]
    top_all[pl.ds(w, 1)] = mine[None]

    def top_copy(i):
        t = top_all.at[w]
        return rcopy(t, t, s_top.at[i], r_top.at[i], wide_peer(i + 1))

    each(W - 1, lambda i: top_copy(i).start())

    each(W - 1, lambda i: req_copy(i).wait_recv())
    req_local = pltpu.make_async_copy(req_in, req_s, l_req)
    req_local.start()

    each(W * N - 1, lambda i: pts_copy(i).wait_recv())

    def features(i):
        a = pts_in[i].astype(F32)
        abc = [a[c * ld : (c + 1) * ld] for c in range(3)]
        anorm = (abc[0] * abc[0] + abc[1] * abc[1] + abc[2] * abc[2]) * SCALE
        one_a = jnp.ones((ld, half), F32)
        arows = [abc[0]] * 3 + [abc[1]] * 3 + [abc[2]] * 3
        arows = arows + pieces(anorm) + [one_a] * 3 + [one_a * 0.0]
        feat[pl.ds(i * ld, ld)] = (
            dot(perm, jnp.concatenate(arows, axis=0).astype(BF16))
            .astype(BF16)
            .reshape(ld, FEATS, half)
        )

    each(W * N, features)
    req_local.wait()

    def wide_copy(i, c):
        return rcopy(
            stage.at[c, i], cand[c].at[pl.ds(block + w * SEND_CAP, SEND_CAP)],
            s_wide.at[c, i], r_wide.at[c, i], wide_peer(i + 1),
        )

    def make_tiles(first, last):
        def step(t, carry):
            b = bfeat[t]
            for k in range(slots):
                a = feat[jnp.maximum(near_s[t, k], 0)]
                s = jnp.maximum(dot(a, b, 0, 0), 1e-30)
                q = s * lax.rsqrt(s)
                tile = (1.0 + LN2 * q) * jnp.exp2(-q)
                tiles[t, k * half : (k + 1) * half, :] = tile.astype(BF16)
            return carry

        lax.fori_loop(first, last, step, 0)

    rank_dim = skel_ref.shape[2]

    def ag_copy(i):
        f = fpiece.at[me]
        return rcopy(f, f, s_ag.at[i], r_ag.at[i], mate(i + 1))

    for c in range(ch):
        each(N - 1, lambda i: nar_copy(i, c).wait_recv())

        def put(i):
            for r in range(SEND_CAP):
                leaf = jnp.clip(req_s[i, r, w], 0, block - 1)
                stage[c, W - 2 - i, r] = loc[c][leaf]

        each(W - 1, put)
        each(W - 1, lambda i: wide_copy(i, c).start())
        cand[c][pl.ds(0, block)] = loc[c][...]
        make_tiles(c * ld // ch, (c + 1) * ld // ch)
        if c != ch // 2:
            continue

        each(W - 1, lambda i: top_copy(i).wait_recv())
        fields = jnp.zeros((pr, rank_dim), F32)
        for k in range(coup_s.shape[1]):
            partner = coup_s[0, k]
            sq = jnp.zeros((rank_dim, rank_dim), F32)
            for x in range(3):
                row = skel_ref[x, pl.ds(partner, 1), :]
                delta = jnp.broadcast_to(row, (rank_dim, rank_dim)).T - skel_ref[x, pl.ds(w, 1), :]
                sq = sq + delta * delta
            q = RATE * jnp.sqrt(sq)
            tile = 0.125 * (1.0 + q) * jnp.exp(-q)
            fields = fields + dot(top_all[partner], tile, precision=HIGH)
        fpiece[pl.ds(me, 1)] = fields[None]
        each(mates - 1, lambda i: ag_copy(i).start())

    each(mates - 1, lambda i: ag_copy(i).wait_recv())
    top = fpiece[...].reshape(cols, rank_dim)
    parent = dot(top, ptc_ref[0], 1, 1, precision=HIGH)
    for l in range(ld):
        lf = dot(parent, lt_ref[l], 1, 1, precision=HIGH).astype(BF16)
        out_ref[l] = vec_ref[l] + dot(lf, basis_ref[l])

    map_copy.wait()

    def near_copy(t):
        return rcopy(near_out.at[t], near_in.at[t], s_near.at[t], r_near.at[t], other)

    for c in range(ch):
        each(W - 1, lambda i: wide_copy(i, c).wait_recv())

    def product(t, carry):
        acc = jnp.zeros((cols, full), F32)
        for k in range(0, slots, 2):
            at = [jnp.clip(map_s[t, k + j], 0, block + W * SEND_CAP - 1) for j in range(2)]
            lhs = jnp.concatenate(
                [jnp.concatenate([cand[c][a] for c in range(ch)], axis=0) for a in at], axis=1
            )
            acc = acc + dot(lhs, tiles[t, k * half : (k + 2) * half, :])
        acc = acc * 0.125
        low, high = acc[:, :half], acc[:, half:]
        near_out[t] = jnp.where(v == 0, high, low).astype(BF16)
        near_copy(t).start()
        out_ref[t] = out_ref[t] + jnp.where(v == 0, low, high)
        return carry

    lax.fori_loop(0, ld, product, 0)

    def finish(t, carry):
        near_copy(t).wait_recv()
        out_ref[t] = out_ref[t] + near_in[t].astype(F32)
        return carry

    lax.fori_loop(0, ld, finish, 0)

    each(W - 1, lambda i: req_copy(i).wait_send())
    each(mates - 1, lambda i: mate_copy(i).wait_send())
    each(W * N - 1, lambda i: pts_copy(i).wait_send())
    each(W - 1, lambda i: top_copy(i).wait_send())
    each(mates - 1, lambda i: ag_copy(i).wait_send())
    each(ld, lambda t: near_copy(t).wait_send())
    for c in range(ch):
        each(N - 1, lambda i: nar_copy(i, c).wait_send())
        each(W - 1, lambda i: wide_copy(i, c).wait_send())


def body(W, N, V, vectors, points, near_list, basis, transfer, ptc, skeleton, coupling):
    ld, cols, half = vectors.shape
    full = points.shape[2]
    slots = near_list.shape[1]
    rank = transfer.shape[1]
    ch = CHUNKS
    cw = cols // ch
    block = ld * N
    mates = N * V
    pr = cols // mates
    prow = -(-3 * ld // 16) * 16
    dma = pltpu.SemaphoreType.DMA
    vmem = pltpu.VMEM
    scratch = [vmem((block, cw, half), BF16)] * ch
    scratch += [vmem((block + W * SEND_CAP, cw, half), BF16)] * ch
    scratch += [
        vmem((ch, W - 1, SEND_CAP, cw, half), BF16),
        vmem((8, 128), I32),
        vmem((W - 1, 8, 128), I32),
        pltpu.SMEM((W - 1, 8, 128), I32),
        vmem((ld, 128), I32),
        pltpu.SMEM((ld, 128), I32),
        vmem((prow, half), BF16),
        vmem((W * N, prow, half), BF16),
        vmem((W * N * ld, FEATS, half), BF16),
        vmem((ld, FEATS, full), BF16),
        vmem((ld, slots * half, full), BF16),
        vmem((mates, pr, rank), F32),
        vmem((mates - 1, pr, rank), F32),
        vmem((W, pr, rank), F32),
        vmem((mates, pr, rank), F32),
        vmem((ld, cols, half), BF16),
        vmem((ld, cols, half), BF16),
    ]
    scratch += [dma((W - 1,))] * 2 + [dma((W * N - 1,))] * 2 + [dma((ch, N - 1))] * 2
    scratch += [dma((ch, W - 1))] * 2 + [dma((mates - 1,))] * 2 + [dma((W - 1,))] * 2
    scratch += [dma((mates - 1,))] * 2 + [dma((ld,))] * 2 + [dma(())] * 2
    in_v = pl.BlockSpec(memory_space=pltpu.VMEM)
    in_s = pl.BlockSpec(memory_space=pltpu.SMEM)
    return pl.pallas_call(
        functools.partial(kernel, W, N, V),
        out_shape=jax.ShapeDtypeStruct(vectors.shape, F32),
        in_specs=[in_v, in_v, in_s, in_v, in_v, in_v, in_v, in_v, in_s],
        out_specs=in_v,
        scratch_shapes=scratch,
        compiler_params=pltpu.CompilerParams(
            collective_id=0, has_side_effects=True, vmem_limit_bytes=56 << 20
        ),
    )(
        vectors, points.transpose(1, 0, 2), near_list, near_list, basis, transfer, ptc,
        skeleton.transpose(1, 0, 2), coupling,
    )


def solution(mesh):
    rows = ("groups", "wide", "narrow")
    in_specs = (
        P(rows, None, "vec"),
        P(rows, None, None),
        P(rows, None),
        P(rows, None, "vec"),
        P(rows, None, None),
        P(rows, None, None),
        P("groups", None, None),
        P(("groups", "wide"), None),
    )
    sizes = [mesh.shape[a] for a in ("wide", "narrow", "vec")]
    return jax.shard_map(
        functools.partial(body, *sizes),
        mesh=mesh,
        in_specs=in_specs,
        out_specs=P(rows, None, "vec"),
        check_vma=False,
    )
```

```python
import functools
import math

import jax
import jax.numpy as jnp
from jax import lax
from jax.experimental import pallas as pl
from jax.experimental.pallas import tpu as pltpu
from jax.sharding import PartitionSpec as P

SEND_CAP = 4
FEATS = 16
CHUNKS = 4

RATE = 8.660254037844386
LOG2E = math.log2(math.e)
LN2 = math.log(2.0)
SCALE = (RATE * LOG2E) ** 2
MESH = pl.DeviceIdType.MESH
HIGH = lax.Precision.HIGHEST
F32, BF16, I32 = jnp.float32, jnp.bfloat16, jnp.int32


def each(count, step):
    if count <= 8:
        for i in range(count):
            step(i)
    else:
        lax.fori_loop(0, count, lambda i, _: (step(i), 0)[1], 0)


def pieces(value):
    first = value.astype(BF16).astype(F32)
    rest = value - first
    second = rest.astype(BF16).astype(F32)
    return [first, second, rest - second]


def dot(a, b, ca=1, cb=0, precision=None):
    return lax.dot_general(
        a, b, (((ca,), (cb,)), ((), ())), precision=precision, preferred_element_type=F32
    )


def kernel(
    W, N, V,
    vec_ref, pts_ref, near_s, near_v, basis_ref, lt_ref, ptc_ref, skel_ref, coup_s,
    out_ref, *scratch,
):
    ch = CHUNKS
    loc, cand, scratch = scratch[:ch], scratch[ch : 2 * ch], scratch[2 * ch :]
    (
        stage, req_out, req_in, req_s, map_v, map_s, pts_out, pts_in, feat, bfeat, tiles,
        term, mate_in, top_all, fpiece, near_out, near_in,
        s_req, r_req, s_pts, r_pts, s_nar, r_nar, s_wide, r_wide,
        s_mate, r_mate, s_top, r_top, s_ag, r_ag, s_near, r_near, l_req, l_map,
    ) = scratch
    ld, cols, half = vec_ref.shape
    full = pts_ref.shape[2]
    slots = near_v.shape[1]
    cw = cols // ch
    block = ld * N
    leaves = W * block
    shift = block.bit_length() - 1
    lp = max(128, leaves)
    mates = N * V
    pr = cols // mates
    w, n, v = lax.axis_index("wide"), lax.axis_index("narrow"), lax.axis_index("vec")
    me = n * V + v

    def mate(d):
        m = lax.rem(me + d, mates)
        return {"narrow": m // V, "vec": m % V}

    def wide_peer(d):
        return {"wide": lax.rem(w + d, W)}

    def narrow_peer(d):
        return {"narrow": lax.rem(n + d, N)}

    spot = w * N + n

    def group_peer(d):
        p = lax.rem(spot + d, W * N)
        return {"wide": p // N, "narrow": p % N}

    other = {"vec": 1 - v}

    def rcopy(src, dst, ss, rs, dev):
        return pltpu.make_async_remote_copy(
            src_ref=src, dst_ref=dst, send_sem=ss, recv_sem=rs, device_id=dev, device_id_type=MESH
        )

    barrier = pltpu.get_barrier_semaphore()

    def greet(fn):
        def step(i):
            pl.semaphore_signal(barrier, inc=1, device_id=fn(i + 1), device_id_type=MESH)
        return step

    each(W * N - 1, greet(group_peer))
    each(mates - 1, greet(mate))

    base = n * ld
    for c in range(ch):
        loc[c][pl.ds(base, ld)] = vec_ref[:, c * cw : (c + 1) * cw, :].astype(BF16)
        cand[c][pl.ds(block + w * SEND_CAP, SEND_CAP)] = jnp.zeros((SEND_CAP, cw, half), BF16)

    nl = near_v[...]
    lane = lax.broadcasted_iota(I32, (ld, lp), 1)
    hits = jnp.zeros((ld, lp), F32)
    for k in range(slots):
        hits = jnp.where(nl[:, k : k + 1] == lane, 1.0, hits)
    mask = jnp.broadcast_to(jnp.max(hits, axis=0, keepdims=True), (8, lp))
    lane8 = lax.broadcasted_iota(I32, (8, lp), 1)
    owner8 = lax.shift_right_logical(lane8, shift)
    mask = jnp.where(owner8 == w, 0.0, mask)
    ti = lax.broadcasted_iota(I32, (lp, lp), 0)
    tj = lax.broadcasted_iota(I32, (lp, lp), 1)
    tri = (ti < tj) & (lax.shift_right_logical(ti, shift) == lax.shift_right_logical(tj, shift))
    rank = dot(mask.astype(BF16), jnp.where(tri, 1.0, 0.0).astype(BF16))
    row8 = lax.broadcasted_iota(I32, (8, lp), 0).astype(F32)
    inner8 = (lane8 & (block - 1)).astype(F32)
    sel = jnp.where((rank == row8) & (mask > 0.5), inner8, 0.0)
    si = lax.broadcasted_iota(I32, (lp, 128), 0)
    sj = lax.broadcasted_iota(I32, (lp, 128), 1)
    seg = jnp.where(lax.shift_right_logical(si, shift) == sj, 1.0, 0.0).astype(BF16)
    req_out[...] = dot(sel.astype(BF16), seg).astype(I32)

    xyz = [pts_ref[c].astype(F32) for c in range(3)]
    halves = [jnp.where(v == 0, a[:, :half], a[:, half:]) for a in xyz]
    prow = pts_out.shape[0]
    pts_out[...] = jnp.concatenate(
        halves + [jnp.zeros((prow - 3 * ld, half), F32)], axis=0
    ).astype(BF16)
    pts_in[pl.ds(spot, 1)] = pts_out[...][None]

    weights = [
        dot(
            jnp.concatenate([loc[c][base + l] for c in range(ch)], axis=0), basis_ref[l], 1, 1
        )
        for l in range(ld)
    ]
    sums = weights[0] * 0.0
    for l in range(ld):
        sums = sums + dot(weights[l], lt_ref[l], precision=HIGH)
    term[...] = dot(sums, ptc_ref[0], precision=HIGH).reshape(mates, pr, -1)

    pl.semaphore_wait(barrier, W * N - 1 + mates - 1)

    def req_copy(i):
        return rcopy(req_out, req_in.at[i], s_req.at[i], r_req.at[i], wide_peer(i + 1))

    def mate_copy(i):
        m = lax.rem(me + i + 1, mates)
        return rcopy(term.at[m], mate_in.at[i], s_mate.at[i], r_mate.at[i], mate(i + 1))

    def pts_copy(i):
        return rcopy(pts_out, pts_in.at[spot], s_pts.at[i], r_pts.at[i], group_peer(i + 1))

    def nar_copy(i, c):
        mine = loc[c].at[pl.ds(base, ld)]
        return rcopy(mine, mine, s_nar.at[c, i], r_nar.at[c, i], narrow_peer(i + 1))

    each(W - 1, lambda i: req_copy(i).start())
    each(mates - 1, lambda i: mate_copy(i).start())
    each(W * N - 1, lambda i: pts_copy(i).start())
    for c in range(ch):
        each(N - 1, lambda i: nar_copy(i, c).start())

    each(W - 1, lambda i: req_copy(i).wait_recv())
    req_local = pltpu.make_async_copy(req_in, req_s, l_req)
    req_local.start()

    each(mates - 1, lambda i: mate_copy(i).wait_recv())
    mine = term[me]
    for i in range(mates - 1):
        mine = mine + mate_in[i]
    top_all[pl.ds(w, 1)] = mine[None]

    def top_copy(i):
        t = top_all.at[w]
        return rcopy(t, t, s_top.at[i], r_top.at[i], wide_peer(i + 1))

    each(W - 1, lambda i: top_copy(i).start())

    req_local.wait()

    def wide_copy(i, c):
        return rcopy(
            stage.at[c, i], cand[c].at[pl.ds(block + w * SEND_CAP, SEND_CAP)],
            s_wide.at[c, i], r_wide.at[c, i], wide_peer(i + 1),
        )

    def make_tiles(first, last):
        def step(t, carry):
            b = bfeat[t]
            for k in range(slots):
                a = feat[jnp.maximum(near_s[t, k], 0)]
                s = jnp.maximum(dot(a, b, 0, 0), 1e-30)
                q = s * lax.rsqrt(s)
                tile = (1.0 + LN2 * q) * jnp.exp2(-q)
                tiles[t, k * half : (k + 1) * half, :] = tile.astype(BF16)
            return carry

        lax.fori_loop(first, last, step, 0)

    rank_dim = skel_ref.shape[2]

    def ag_copy(i):
        f = fpiece.at[me]
        return rcopy(f, f, s_ag.at[i], r_ag.at[i], mate(i + 1))

    def prepare():
        owner_l = lax.shift_right_logical(lane, shift)
        place = jnp.where(
            owner_l == w,
            (lane - w * block).astype(F32),
            (block + owner_l * SEND_CAP).astype(F32) + jnp.broadcast_to(rank[:1], (ld, lp)),
        )
        mlane = lax.broadcasted_iota(I32, (ld, 128), 1)
        found = jnp.zeros((ld, 128), F32)
        zero_slot = (block + w * SEND_CAP).astype(F32)
        for k in range(slots):
            entry = nl[:, k : k + 1]
            at = jnp.sum(jnp.where(entry == lane, place, 0.0), axis=1, keepdims=True)
            at = jnp.where(entry >= 0, at, zero_slot)
            found = jnp.where(mlane == k, at, found)
        map_v[...] = found.astype(I32)
        map_copy = pltpu.make_async_copy(map_v, map_s, l_map)
        map_copy.start()

        rows = ld * FEATS
        pi = lax.broadcasted_iota(I32, (rows, rows), 0)
        pj = lax.broadcasted_iota(I32, (rows, rows), 1)
        fshift = FEATS.bit_length() - 1
        perm = pj == (pi & (FEATS - 1)) * ld + lax.shift_right_logical(pi, fshift)
        perm = jnp.where(perm, 1.0, 0.0).astype(BF16)
        one_b = jnp.ones((ld, full), F32)
        norm = (xyz[0] * xyz[0] + xyz[1] * xyz[1] + xyz[2] * xyz[2]) * SCALE
        brows = sum((pieces(a * (-2.0 * SCALE)) for a in xyz), [])
        brows = brows + [one_b] * 3 + pieces(norm) + [one_b * 0.0]
        bfeat[...] = (
            dot(perm, jnp.concatenate(brows, axis=0).astype(BF16))
            .astype(BF16)
            .reshape(ld, FEATS, full)
        )

        each(W * N - 1, lambda i: pts_copy(i).wait_recv())

        def features(i):
            a = pts_in[i].astype(F32)
            abc = [a[c * ld : (c + 1) * ld] for c in range(3)]
            anorm = (abc[0] * abc[0] + abc[1] * abc[1] + abc[2] * abc[2]) * SCALE
            one_a = jnp.ones((ld, half), F32)
            arows = [abc[0]] * 3 + [abc[1]] * 3 + [abc[2]] * 3
            arows = arows + pieces(anorm) + [one_a] * 3 + [one_a * 0.0]
            feat[pl.ds(i * ld, ld)] = (
                dot(perm, jnp.concatenate(arows, axis=0).astype(BF16))
                .astype(BF16)
                .reshape(ld, FEATS, half)
            )

        each(W * N, features)
        return map_copy

    for c in range(ch):
        each(N - 1, lambda i: nar_copy(i, c).wait_recv())

        def put(i):
            for r in range(SEND_CAP):
                leaf = jnp.clip(req_s[i, r, w], 0, block - 1)
                stage[c, W - 2 - i, r] = loc[c][leaf]

        each(W - 1, put)
        each(W - 1, lambda i: wide_copy(i, c).start())
        if c == 0:
            map_copy = prepare()
        cand[c][pl.ds(0, block)] = loc[c][...]
        make_tiles(c * ld // ch, (c + 1) * ld // ch)
        if c != ch // 2:
            continue

        each(W - 1, lambda i: top_copy(i).wait_recv())
        fields = jnp.zeros((pr, rank_dim), F32)
        for k in range(coup_s.shape[1]):
            partner = coup_s[0, k]
            sq = jnp.zeros((rank_dim, rank_dim), F32)
            for x in range(3):
                row = skel_ref[x, pl.ds(partner, 1), :]
                delta = jnp.broadcast_to(row, (rank_dim, rank_dim)).T - skel_ref[x, pl.ds(w, 1), :]
                sq = sq + delta * delta
            q = RATE * jnp.sqrt(sq)
            tile = 0.125 * (1.0 + q) * jnp.exp(-q)
            fields = fields + dot(top_all[partner], tile, precision=HIGH)
        fpiece[pl.ds(me, 1)] = fields[None]
        each(mates - 1, lambda i: ag_copy(i).start())

    each(mates - 1, lambda i: ag_copy(i).wait_recv())
    top = fpiece[...].reshape(cols, rank_dim)
    parent = dot(top, ptc_ref[0], 1, 1, precision=HIGH)
    for l in range(ld):
        lf = dot(parent, lt_ref[l], 1, 1, precision=HIGH).astype(BF16)
        out_ref[l] = vec_ref[l] + dot(lf, basis_ref[l])

    map_copy.wait()

    def near_copy(t):
        return rcopy(near_out.at[t], near_in.at[t], s_near.at[t], r_near.at[t], other)

    for c in range(ch):
        each(W - 1, lambda i: wide_copy(i, c).wait_recv())

    def product(t, carry):
        acc = jnp.zeros((cols, full), F32)
        for k in range(0, slots, 2):
            at = [jnp.clip(map_s[t, k + j], 0, block + W * SEND_CAP - 1) for j in range(2)]
            lhs = jnp.concatenate(
                [jnp.concatenate([cand[c][a] for c in range(ch)], axis=0) for a in at], axis=1
            )
            acc = acc + dot(lhs, tiles[t, k * half : (k + 2) * half, :])
        acc = acc * 0.125
        low, high = acc[:, :half], acc[:, half:]
        near_out[t] = jnp.where(v == 0, high, low).astype(BF16)
        near_copy(t).start()
        out_ref[t] = out_ref[t] + jnp.where(v == 0, low, high)
        return carry

    lax.fori_loop(0, ld, product, 0)

    def finish(t, carry):
        near_copy(t).wait_recv()
        out_ref[t] = out_ref[t] + near_in[t].astype(F32)
        return carry

    lax.fori_loop(0, ld, finish, 0)

    each(W - 1, lambda i: req_copy(i).wait_send())
    each(mates - 1, lambda i: mate_copy(i).wait_send())
    each(W * N - 1, lambda i: pts_copy(i).wait_send())
    each(W - 1, lambda i: top_copy(i).wait_send())
    each(mates - 1, lambda i: ag_copy(i).wait_send())
    each(ld, lambda t: near_copy(t).wait_send())
    for c in range(ch):
        each(N - 1, lambda i: nar_copy(i, c).wait_send())
        each(W - 1, lambda i: wide_copy(i, c).wait_send())


def body(W, N, V, vectors, points, near_list, basis, transfer, ptc, skeleton, coupling):
    ld, cols, half = vectors.shape
    full = points.shape[2]
    slots = near_list.shape[1]
    rank = transfer.shape[1]
    ch = CHUNKS
    cw = cols // ch
    block = ld * N
    mates = N * V
    pr = cols // mates
    prow = -(-3 * ld // 16) * 16
    dma = pltpu.SemaphoreType.DMA
    vmem = pltpu.VMEM
    scratch = [vmem((block, cw, half), BF16)] * ch
    scratch += [vmem((block + W * SEND_CAP, cw, half), BF16)] * ch
    scratch += [
        vmem((ch, W - 1, SEND_CAP, cw, half), BF16),
        vmem((8, 128), I32),
        vmem((W - 1, 8, 128), I32),
        pltpu.SMEM((W - 1, 8, 128), I32),
        vmem((ld, 128), I32),
        pltpu.SMEM((ld, 128), I32),
        vmem((prow, half), BF16),
        vmem((W * N, prow, half), BF16),
        vmem((W * N * ld, FEATS, half), BF16),
        vmem((ld, FEATS, full), BF16),
        vmem((ld, slots * half, full), BF16),
        vmem((mates, pr, rank), F32),
        vmem((mates - 1, pr, rank), F32),
        vmem((W, pr, rank), F32),
        vmem((mates, pr, rank), F32),
        vmem((ld, cols, half), BF16),
        vmem((ld, cols, half), BF16),
    ]
    scratch += [dma((W - 1,))] * 2 + [dma((W * N - 1,))] * 2 + [dma((ch, N - 1))] * 2
    scratch += [dma((ch, W - 1))] * 2 + [dma((mates - 1,))] * 2 + [dma((W - 1,))] * 2
    scratch += [dma((mates - 1,))] * 2 + [dma((ld,))] * 2 + [dma(())] * 2
    in_v = pl.BlockSpec(memory_space=pltpu.VMEM)
    in_s = pl.BlockSpec(memory_space=pltpu.SMEM)
    return pl.pallas_call(
        functools.partial(kernel, W, N, V),
        out_shape=pltpu.VMEM(vectors.shape, F32),
        in_specs=[in_v, in_v, in_s, in_v, in_v, in_v, in_v, in_v, in_s],
        out_specs=in_v,
        scratch_shapes=scratch,
        compiler_params=pltpu.CompilerParams(
            collective_id=0, has_side_effects=True, vmem_limit_bytes=56 << 20
        ),
    )(
        vectors, points.transpose(1, 0, 2), near_list, near_list, basis, transfer, ptc,
        skeleton.transpose(1, 0, 2), coupling,
    )


def solution(mesh):
    rows = ("groups", "wide", "narrow")
    in_specs = (
        P(rows, None, "vec"),
        P(rows, None, None),
        P(rows, None),
        P(rows, None, "vec"),
        P(rows, None, None),
        P(rows, None, None),
        P("groups", None, None),
        P(("groups", "wide"), None),
    )
    sizes = [mesh.shape[a] for a in ("wide", "narrow", "vec")]
    return jax.shard_map(
        functools.partial(body, *sizes),
        mesh=mesh,
        in_specs=in_specs,
        out_specs=P(rows, None, "vec"),
        check_vma=False,
    )
```

```python
import functools
import math

import jax
import jax.numpy as jnp
from jax import lax
from jax.experimental import pallas as pl
from jax.experimental.pallas import tpu as pltpu
from jax.sharding import PartitionSpec as P

SEND_CAP = 4
FEATS = 16
CHUNKS = 4

RATE = 8.660254037844386
LOG2E = math.log2(math.e)
LN2 = math.log(2.0)
SCALE = (RATE * LOG2E) ** 2
MESH = pl.DeviceIdType.MESH
HIGH = lax.Precision.HIGHEST
F32, BF16, I32 = jnp.float32, jnp.bfloat16, jnp.int32


def each(count, step):
    if count <= 8:
        for i in range(count):
            step(i)
    else:
        lax.fori_loop(0, count, lambda i, _: (step(i), 0)[1], 0)


def pieces(value):
    first = value.astype(BF16).astype(F32)
    rest = value - first
    second = rest.astype(BF16).astype(F32)
    return [first, second, rest - second]


def dot(a, b, ca=1, cb=0, precision=None):
    return lax.dot_general(
        a, b, (((ca,), (cb,)), ((), ())), precision=precision, preferred_element_type=F32
    )


def kernel(
    W, N, V,
    *refs,
):
    ch = CHUNKS
    args, out_ref, here, scratch = refs[:9], refs[9], refs[10:19], refs[19:]
    vec_ref, pts_ref, near_s, near_v, basis_ref, lt_ref, ptc_ref, skel_ref, coup_s = here
    loc, cand, scratch = scratch[:ch], scratch[ch : 2 * ch], scratch[2 * ch :]
    (
        stage, req_out, req_in, req_s, map_v, map_s, pts_out, pts_in, feat, bfeat, tiles,
        term, mate_in, top_all, fpiece, near_out, near_in,
        s_req, r_req, s_pts, r_pts, s_nar, r_nar, s_wide, r_wide,
        s_mate, r_mate, s_top, r_top, s_ag, r_ag, s_near, r_near, l_req, l_map, l_in,
    ) = scratch
    ld, cols, half = vec_ref.shape
    full = pts_ref.shape[2]
    slots = near_v.shape[1]
    cw = cols // ch
    block = ld * N
    leaves = W * block
    shift = block.bit_length() - 1
    lp = max(128, leaves)
    mates = N * V
    pr = cols // mates
    w, n, v = lax.axis_index("wide"), lax.axis_index("narrow"), lax.axis_index("vec")
    me = n * V + v

    def mate(d):
        m = lax.rem(me + d, mates)
        return {"narrow": m // V, "vec": m % V}

    def wide_peer(d):
        return {"wide": lax.rem(w + d, W)}

    def narrow_peer(d):
        return {"narrow": lax.rem(n + d, N)}

    spot = w * N + n

    def group_peer(d):
        p = lax.rem(spot + d, W * N)
        return {"wide": p // N, "narrow": p % N}

    other = {"vec": 1 - v}

    def rcopy(src, dst, ss, rs, dev):
        return pltpu.make_async_remote_copy(
            src_ref=src, dst_ref=dst, send_sem=ss, recv_sem=rs, device_id=dev, device_id_type=MESH
        )

    barrier = pltpu.get_barrier_semaphore()

    def greet(fn):
        def step(i):
            pl.semaphore_signal(barrier, inc=1, device_id=fn(i + 1), device_id_type=MESH)
        return step

    each(W * N - 1, greet(group_peer))
    each(mates - 1, greet(mate))

    fetch = [pltpu.make_async_copy(a, h, l_in.at[i]) for i, (a, h) in enumerate(zip(args, here))]
    for i in (3, 0, 1, 4, 5, 6, 2, 7, 8):
        fetch[i].start()
    fetch[0].wait()

    base = n * ld
    for c in range(ch):
        loc[c][pl.ds(base, ld)] = vec_ref[:, c * cw : (c + 1) * cw, :].astype(BF16)
        cand[c][pl.ds(block + w * SEND_CAP, SEND_CAP)] = jnp.zeros((SEND_CAP, cw, half), BF16)

    fetch[3].wait()
    nl = near_v[...]
    lane = lax.broadcasted_iota(I32, (ld, lp), 1)
    hits = jnp.zeros((ld, lp), F32)
    for k in range(slots):
        hits = jnp.where(nl[:, k : k + 1] == lane, 1.0, hits)
    mask = jnp.broadcast_to(jnp.max(hits, axis=0, keepdims=True), (8, lp))
    lane8 = lax.broadcasted_iota(I32, (8, lp), 1)
    owner8 = lax.shift_right_logical(lane8, shift)
    mask = jnp.where(owner8 == w, 0.0, mask)
    ti = lax.broadcasted_iota(I32, (lp, lp), 0)
    tj = lax.broadcasted_iota(I32, (lp, lp), 1)
    tri = (ti < tj) & (lax.shift_right_logical(ti, shift) == lax.shift_right_logical(tj, shift))
    rank = dot(mask.astype(BF16), jnp.where(tri, 1.0, 0.0).astype(BF16))
    row8 = lax.broadcasted_iota(I32, (8, lp), 0).astype(F32)
    inner8 = (lane8 & (block - 1)).astype(F32)
    sel = jnp.where((rank == row8) & (mask > 0.5), inner8, 0.0)
    si = lax.broadcasted_iota(I32, (lp, 128), 0)
    sj = lax.broadcasted_iota(I32, (lp, 128), 1)
    seg = jnp.where(lax.shift_right_logical(si, shift) == sj, 1.0, 0.0).astype(BF16)
    req_out[...] = dot(sel.astype(BF16), seg).astype(I32)

    fetch[1].wait()
    xyz = [pts_ref[c].astype(F32) for c in range(3)]
    halves = [jnp.where(v == 0, a[:, :half], a[:, half:]) for a in xyz]
    prow = pts_out.shape[0]
    pts_out[...] = jnp.concatenate(
        halves + [jnp.zeros((prow - 3 * ld, half), F32)], axis=0
    ).astype(BF16)
    pts_in[pl.ds(spot, 1)] = pts_out[...][None]

    for i in (4, 5, 6, 2, 7, 8):
        fetch[i].wait()
    weights = [
        dot(
            jnp.concatenate([loc[c][base + l] for c in range(ch)], axis=0), basis_ref[l], 1, 1
        )
        for l in range(ld)
    ]
    sums = weights[0] * 0.0
    for l in range(ld):
        sums = sums + dot(weights[l], lt_ref[l], precision=HIGH)
    term[...] = dot(sums, ptc_ref[0], precision=HIGH).reshape(mates, pr, -1)

    pl.semaphore_wait(barrier, W * N - 1 + mates - 1)

    def req_copy(i):
        return rcopy(req_out, req_in.at[i], s_req.at[i], r_req.at[i], wide_peer(i + 1))

    def mate_copy(i):
        m = lax.rem(me + i + 1, mates)
        return rcopy(term.at[m], mate_in.at[i], s_mate.at[i], r_mate.at[i], mate(i + 1))

    def pts_copy(i):
        return rcopy(pts_out, pts_in.at[spot], s_pts.at[i], r_pts.at[i], group_peer(i + 1))

    def nar_copy(i, c):
        mine = loc[c].at[pl.ds(base, ld)]
        return rcopy(mine, mine, s_nar.at[c, i], r_nar.at[c, i], narrow_peer(i + 1))

    each(W - 1, lambda i: req_copy(i).start())
    each(mates - 1, lambda i: mate_copy(i).start())
    each(W * N - 1, lambda i: pts_copy(i).start())
    for c in range(ch):
        each(N - 1, lambda i: nar_copy(i, c).start())

    each(W - 1, lambda i: req_copy(i).wait_recv())
    req_local = pltpu.make_async_copy(req_in, req_s, l_req)
    req_local.start()

    each(mates - 1, lambda i: mate_copy(i).wait_recv())
    mine = term[me]
    for i in range(mates - 1):
        mine = mine + mate_in[i]
    top_all[pl.ds(w, 1)] = mine[None]

    def top_copy(i):
        t = top_all.at[w]
        return rcopy(t, t, s_top.at[i], r_top.at[i], wide_peer(i + 1))

    each(W - 1, lambda i: top_copy(i).start())

    req_local.wait()

    def wide_copy(i, c):
        return rcopy(
            stage.at[c, i], cand[c].at[pl.ds(block + w * SEND_CAP, SEND_CAP)],
            s_wide.at[c, i], r_wide.at[c, i], wide_peer(i + 1),
        )

    def make_tiles(first, last):
        def step(t, carry):
            b = bfeat[t]
            for k in range(slots):
                a = feat[jnp.maximum(near_s[t, k], 0)]
                s = jnp.maximum(dot(a, b, 0, 0), 1e-30)
                q = s * lax.rsqrt(s)
                tile = (1.0 + LN2 * q) * jnp.exp2(-q)
                tiles[t, k * half : (k + 1) * half, :] = tile.astype(BF16)
            return carry

        lax.fori_loop(first, last, step, 0)

    rank_dim = skel_ref.shape[2]

    def ag_copy(i):
        f = fpiece.at[me]
        return rcopy(f, f, s_ag.at[i], r_ag.at[i], mate(i + 1))

    def prepare():
        owner_l = lax.shift_right_logical(lane, shift)
        place = jnp.where(
            owner_l == w,
            (lane - w * block).astype(F32),
            (block + owner_l * SEND_CAP).astype(F32) + jnp.broadcast_to(rank[:1], (ld, lp)),
        )
        mlane = lax.broadcasted_iota(I32, (ld, 128), 1)
        found = jnp.zeros((ld, 128), F32)
        zero_slot = (block + w * SEND_CAP).astype(F32)
        for k in range(slots):
            entry = nl[:, k : k + 1]
            at = jnp.sum(jnp.where(entry == lane, place, 0.0), axis=1, keepdims=True)
            at = jnp.where(entry >= 0, at, zero_slot)
            found = jnp.where(mlane == k, at, found)
        map_v[...] = found.astype(I32)
        map_copy = pltpu.make_async_copy(map_v, map_s, l_map)
        map_copy.start()

        rows = ld * FEATS
        pi = lax.broadcasted_iota(I32, (rows, rows), 0)
        pj = lax.broadcasted_iota(I32, (rows, rows), 1)
        fshift = FEATS.bit_length() - 1
        perm = pj == (pi & (FEATS - 1)) * ld + lax.shift_right_logical(pi, fshift)
        perm = jnp.where(perm, 1.0, 0.0).astype(BF16)
        one_b = jnp.ones((ld, full), F32)
        norm = (xyz[0] * xyz[0] + xyz[1] * xyz[1] + xyz[2] * xyz[2]) * SCALE
        brows = sum((pieces(a * (-2.0 * SCALE)) for a in xyz), [])
        brows = brows + [one_b] * 3 + pieces(norm) + [one_b * 0.0]
        bfeat[...] = (
            dot(perm, jnp.concatenate(brows, axis=0).astype(BF16))
            .astype(BF16)
            .reshape(ld, FEATS, full)
        )

        each(W * N - 1, lambda i: pts_copy(i).wait_recv())

        def features(i):
            a = pts_in[i].astype(F32)
            abc = [a[c * ld : (c + 1) * ld] for c in range(3)]
            anorm = (abc[0] * abc[0] + abc[1] * abc[1] + abc[2] * abc[2]) * SCALE
            one_a = jnp.ones((ld, half), F32)
            arows = [abc[0]] * 3 + [abc[1]] * 3 + [abc[2]] * 3
            arows = arows + pieces(anorm) + [one_a] * 3 + [one_a * 0.0]
            feat[pl.ds(i * ld, ld)] = (
                dot(perm, jnp.concatenate(arows, axis=0).astype(BF16))
                .astype(BF16)
                .reshape(ld, FEATS, half)
            )

        each(W * N, features)
        return map_copy

    for c in range(ch):
        each(N - 1, lambda i: nar_copy(i, c).wait_recv())

        def put(i):
            for r in range(SEND_CAP):
                leaf = jnp.clip(req_s[i, r, w], 0, block - 1)
                stage[c, W - 2 - i, r] = loc[c][leaf]

        each(W - 1, put)
        each(W - 1, lambda i: wide_copy(i, c).start())
        if c == 0:
            map_copy = prepare()
        cand[c][pl.ds(0, block)] = loc[c][...]
        make_tiles(c * ld // ch, (c + 1) * ld // ch)
        if c != ch // 2:
            continue

        each(W - 1, lambda i: top_copy(i).wait_recv())
        fields = jnp.zeros((pr, rank_dim), F32)
        for k in range(coup_s.shape[1]):
            partner = coup_s[0, k]
            sq = jnp.zeros((rank_dim, rank_dim), F32)
            for x in range(3):
                row = skel_ref[x, pl.ds(partner, 1), :]
                delta = jnp.broadcast_to(row, (rank_dim, rank_dim)).T - skel_ref[x, pl.ds(w, 1), :]
                sq = sq + delta * delta
            q = RATE * jnp.sqrt(sq)
            tile = 0.125 * (1.0 + q) * jnp.exp(-q)
            fields = fields + dot(top_all[partner], tile, precision=HIGH)
        fpiece[pl.ds(me, 1)] = fields[None]
        each(mates - 1, lambda i: ag_copy(i).start())

    each(mates - 1, lambda i: ag_copy(i).wait_recv())
    top = fpiece[...].reshape(cols, rank_dim)
    parent = dot(top, ptc_ref[0], 1, 1, precision=HIGH)
    for l in range(ld):
        lf = dot(parent, lt_ref[l], 1, 1, precision=HIGH).astype(BF16)
        out_ref[l] = vec_ref[l] + dot(lf, basis_ref[l])

    map_copy.wait()

    def near_copy(t):
        return rcopy(near_out.at[t], near_in.at[t], s_near.at[t], r_near.at[t], other)

    for c in range(ch):
        each(W - 1, lambda i: wide_copy(i, c).wait_recv())

    def product(t, carry):
        acc = jnp.zeros((cols, full), F32)
        for k in range(0, slots, 2):
            at = [jnp.clip(map_s[t, k + j], 0, block + W * SEND_CAP - 1) for j in range(2)]
            lhs = jnp.concatenate(
                [jnp.concatenate([cand[c][a] for c in range(ch)], axis=0) for a in at], axis=1
            )
            acc = acc + dot(lhs, tiles[t, k * half : (k + 2) * half, :])
        acc = acc * 0.125
        low, high = acc[:, :half], acc[:, half:]
        near_out[t] = jnp.where(v == 0, high, low).astype(BF16)
        near_copy(t).start()
        out_ref[t] = out_ref[t] + jnp.where(v == 0, low, high)
        return carry

    lax.fori_loop(0, ld, product, 0)

    def finish(t, carry):
        near_copy(t).wait_recv()
        out_ref[t] = out_ref[t] + near_in[t].astype(F32)
        return carry

    lax.fori_loop(0, ld, finish, 0)

    each(W - 1, lambda i: req_copy(i).wait_send())
    each(mates - 1, lambda i: mate_copy(i).wait_send())
    each(W * N - 1, lambda i: pts_copy(i).wait_send())
    each(W - 1, lambda i: top_copy(i).wait_send())
    each(mates - 1, lambda i: ag_copy(i).wait_send())
    each(ld, lambda t: near_copy(t).wait_send())
    for c in range(ch):
        each(N - 1, lambda i: nar_copy(i, c).wait_send())
        each(W - 1, lambda i: wide_copy(i, c).wait_send())


def body(W, N, V, vectors, points, near_list, basis, transfer, ptc, skeleton, coupling):
    ld, cols, half = vectors.shape
    full = points.shape[2]
    slots = near_list.shape[1]
    rank = transfer.shape[1]
    ch = CHUNKS
    cw = cols // ch
    block = ld * N
    mates = N * V
    pr = cols // mates
    prow = -(-3 * ld // 16) * 16
    dma = pltpu.SemaphoreType.DMA
    vmem = pltpu.VMEM
    operands = (
        vectors, points.transpose(1, 0, 2), near_list, near_list, basis, transfer, ptc,
        skeleton.transpose(1, 0, 2), coupling,
    )
    scratch = [
        (pltpu.SMEM if i in (2, 8) else vmem)(a.shape, a.dtype) for i, a in enumerate(operands)
    ]
    scratch += [vmem((block, cw, half), BF16)] * ch
    scratch += [vmem((block + W * SEND_CAP, cw, half), BF16)] * ch
    scratch += [
        vmem((ch, W - 1, SEND_CAP, cw, half), BF16),
        vmem((8, 128), I32),
        vmem((W - 1, 8, 128), I32),
        pltpu.SMEM((W - 1, 8, 128), I32),
        vmem((ld, 128), I32),
        pltpu.SMEM((ld, 128), I32),
        vmem((prow, half), BF16),
        vmem((W * N, prow, half), BF16),
        vmem((W * N * ld, FEATS, half), BF16),
        vmem((ld, FEATS, full), BF16),
        vmem((ld, slots * half, full), BF16),
        vmem((mates, pr, rank), F32),
        vmem((mates - 1, pr, rank), F32),
        vmem((W, pr, rank), F32),
        vmem((mates, pr, rank), F32),
        vmem((ld, cols, half), BF16),
        vmem((ld, cols, half), BF16),
    ]
    scratch += [dma((W - 1,))] * 2 + [dma((W * N - 1,))] * 2 + [dma((ch, N - 1))] * 2
    scratch += [dma((ch, W - 1))] * 2 + [dma((mates - 1,))] * 2 + [dma((W - 1,))] * 2
    scratch += [dma((mates - 1,))] * 2 + [dma((ld,))] * 2 + [dma(())] * 2 + [dma((9,))]
    return pl.pallas_call(
        functools.partial(kernel, W, N, V),
        out_shape=pltpu.VMEM(vectors.shape, F32),
        in_specs=[pl.BlockSpec(memory_space=pl.ANY)] * 9,
        out_specs=pl.BlockSpec(memory_space=pltpu.VMEM),
        scratch_shapes=scratch,
        compiler_params=pltpu.CompilerParams(
            collective_id=0, has_side_effects=True, vmem_limit_bytes=56 << 20
        ),
    )(*operands)


def solution(mesh):
    rows = ("groups", "wide", "narrow")
    in_specs = (
        P(rows, None, "vec"),
        P(rows, None, None),
        P(rows, None),
        P(rows, None, "vec"),
        P(rows, None, None),
        P(rows, None, None),
        P("groups", None, None),
        P(("groups", "wide"), None),
    )
    sizes = [mesh.shape[a] for a in ("wide", "narrow", "vec")]
    return jax.shard_map(
        functools.partial(body, *sizes),
        mesh=mesh,
        in_specs=in_specs,
        out_specs=P(rows, None, "vec"),
        check_vma=False,
    )
```
